256 devices in a mesh: row: 8 (over y, core), col: 32 (over x, z).
Axes of the slice: x: 4, y: 4, z: 8, core: 2. Of those that a mesh axis runs over, the one named last changes fastest.
Arguments:
- history: bfloat16 [2, 2, 512, 32, 16384], P(None, None, 'row', None, 'col'), may hold values from -6 to 6
- sigma_rows: bfloat16 [2, 2, 32, 16384], P(None, None, None, 'row'), may hold values from -0.03125 to 0.03125
- propagator: bfloat16 [2, 32, 32], replicated, may hold values from -0.75 to 0.75
- block_map: int32 [64], replicated, may hold values from 0 to 63, each once
- step_index: int32 [1], replicated, may hold values from 1 to 510
Outputs:
- new_rows: float32 [2, 2, 2, 32, 16384], P(None, None, None, None, 'col')
- mirror: bfloat16 [2, 2, 2, 512, 1024], P(None, None, None, 'row')
The draws below stay inside these ranges and needn't reach their ends.
Inputs may be any that keep to these rules, and one draw needn't show every extreme that they name: block_map is a permutation of the 64 time blocks.
All inputs are finite; a program needn't handle non-finite values.
Results may differ from the reference program's by a relative error of at most 0.009.
Values may be sent and summed in bfloat16 or wider, within the bound.
No kernel may reach another device: no remote copies, remote signals or barrier semaphores. Data moves between devices by JAX's collectives and lax.ppermute only.
A program may use at most 64 MiB of HBM per device.

```python
import jax
import jax.numpy as jnp
from jax import lax

ORB = 32
TB = 8
NT = 512
NBLK = 64


def block_levels(stream_key, extent, pieces, smallest, high):
    factor_of = 1.0
    for dim, blocks in pieces:
        draws = jax.random.uniform(jax.random.fold_in(jax.random.fold_in(stream_key, 6), dim), (blocks,), jnp.float32, smallest / len(pieces), high / len(pieces))
        factor_of = factor_of * jnp.repeat(jnp.exp(draws), extent[dim] // blocks).reshape((-1,) + (1,) * (len(extent) - 1 - dim))
    return factor_of


def bell_draw(own_key, extent, width, most, shards=(), held_as=jnp.bfloat16):
    result = jax.random.normal(own_key, extent, jnp.float32) * width
    if len(shards) > 0:
        result = block_levels(own_key, extent, shards, -0.22, 0.18) * result
    return jnp.clip(result, min=-most, max=most).astype(held_as)


def setup_inputs(seed: int = 0) -> dict:
    seeds = jax.random.split(jax.random.key(seed), 6)
    return {
        "history": bell_draw(seeds[0], (2, 2, NT, ORB, NT * ORB), 1.0, 6.0, ((2, 8), (4, 32))),
        "sigma_rows": bell_draw(seeds[1], (2, 2, ORB, NT * ORB), (2 * NT * ORB) ** -0.5, 0.03125, ((3, 8),)),
        "propagator": bell_draw(seeds[2], (2, ORB, ORB), (2 * ORB) ** -0.5, 0.75),
        "block_map": jax.random.permutation(seeds[3], NBLK).astype(jnp.int32),
        "step_index": jax.random.randint(seeds[4], (1,), 1, NT - 1).astype(jnp.int32),
    }


def stacked_rows(real_part, imag_part):
    upper_half = jnp.concatenate([real_part, -imag_part], axis=-1)
    lower_half = jnp.concatenate([imag_part, real_part], axis=-1)
    return jnp.concatenate([upper_half, lower_half], axis=-2)


def turn_back(values):
    return jnp.stack([values[:, 1], -values[:, 0]], axis=1)


def apply_matrix(matrix, row_data):
    kinds = row_data.shape[0]
    flat = row_data.reshape(kinds, matrix.shape[1], row_data.shape[-1])
    outputs = [jnp.dot(matrix, flat[kind_index], preferred_element_type=jnp.float32) for kind_index in range(kinds)]
    return jnp.stack(outputs).reshape(row_data.shape)


def step_weights(time_rows, current):
    beyond = time_rows > current
    edge_one = (time_rows == 0) | (time_rows == current)
    weight_one = jnp.where(beyond, 0.0, jnp.where(edge_one, 0.5, 1.0))
    weight_two = jnp.where(beyond, 0.0, jnp.where(time_rows == 0, 0.5, 1.0))
    return jnp.stack([weight_one, weight_two]).astype(jnp.bfloat16)


def reference(history, sigma_rows, propagator, block_map, step_index):
    current = step_index[0]
    offsets = jnp.arange(TB, dtype=jnp.int32)
    stored_times = (block_map[:, None] * TB + offsets[None, :]).reshape(-1).astype(jnp.int32)
    weights = jnp.repeat(step_weights(stored_times, current), ORB, axis=1)
    weighted = sigma_rows * weights[:, None, None, :]
    stacked = stacked_rows(weighted[:, 0], weighted[:, 1]).reshape(4 * ORB, 2 * NT * ORB)
    products = []
    for kind_index in range(2):
        flat = history[kind_index].reshape(2 * NT * ORB, NT * ORB)
        products.append(jnp.dot(stacked, flat, preferred_element_type=jnp.float32))
    products = jnp.stack(products).reshape(2, 2, 2, ORB, NT * ORB)
    block_slots = jnp.arange(NBLK, dtype=jnp.int32)

    def position(time_value):
        home_block = jnp.sum(jnp.where(block_map == time_value // TB, block_slots, 0)).astype(jnp.int32)
        return (home_block * TB + time_value % TB).astype(jnp.int32)

    propagate = stacked_rows(propagator[0], propagator[1])
    now_row = lax.dynamic_index_in_dim(history, position(current), 2, keepdims=False)
    new_first = apply_matrix(propagate, now_row) + turn_back(products[:, 0])
    first_low = new_first.astype(jnp.bfloat16)
    diagonal = lax.dynamic_slice_in_dim(sigma_rows[1], position(current + 1) * ORB, ORB, 2)
    half_diagonal = diagonal * 0.5
    diag_term = apply_matrix(stacked_rows(half_diagonal[0], half_diagonal[1]), first_low)
    new_second = apply_matrix(propagate, first_low) + turn_back(products[:, 1] + diag_term)
    new_rows = jnp.stack([new_first, new_second])
    flipped = new_rows.astype(jnp.bfloat16).reshape(8, ORB, NT, ORB).transpose(0, 2, 3, 1).reshape(8, NT, ORB * ORB)
    flip_signs = jnp.tile(jnp.array([-1.0, 1.0], jnp.bfloat16), 4)
    mirrored = flipped * flip_signs[:, None, None]
    mirror = jnp.take(mirrored, stored_times, axis=1).reshape(2, 2, 2, NT, ORB * ORB)
    return new_rows, mirror
```

```python
import jax
import jax.numpy as jnp
from jax import lax
from jax.experimental import pallas as pl
from jax.experimental.pallas import tpu as pltpu
from jax.sharding import Mesh, PartitionSpec as P

TB = 8
ORB = 32
ROWS = 8
XS = 4
ZS = 8
BF = jnp.bfloat16
F32 = jnp.float32
SLICES = ROWS * XS
DATA = 32
DIAG = 16
BACK = 160


def dot(a, b):
    return jnp.dot(a, b, preferred_element_type=F32)


def dot_nt(a, b):
    return lax.dot_general(a, b, (((1,), (1,)), ((), ())), preferred_element_type=F32)


def iota(shape, axis):
    return lax.broadcasted_iota(jnp.int32, shape, axis)


def one_hot(cond):
    return jnp.where(cond, 1.0, 0.0).astype(BF)


def product_kernel(map_ref, step_ref, hist_ref, sigma_ref, prop_ref, out_ref, acc_ref, diag_ref):
    k = pl.program_id(0)
    row = lax.axis_index("row")
    current = step_ref[0]
    block = map_ref[row * ROWS + k]

    @pl.when(k == 0)
    def _():
        diag_ref[...] = jnp.zeros_like(diag_ref)

    times = block * TB + iota((1, TB * ORB), 1) // ORB
    beyond = times > current
    weight_two = jnp.where(beyond, 0.0, jnp.where(times == 0, 0.5, 1.0))
    weight_one = jnp.where(beyond, 0.0, jnp.where((times == 0) | (times == current), 0.5, 1.0))
    on_real, on_imag = [], []
    for s, weight in enumerate((weight_one, weight_two)):
        real = sigma_ref[s, 0].astype(F32) * weight
        imag = sigma_ref[s, 1].astype(F32) * weight
        on_real += [imag, -real]
        on_imag += [real, imag]
    left = jnp.concatenate(
        [jnp.concatenate(on_real, axis=0), jnp.concatenate(on_imag, axis=0)], axis=1
    ).astype(BF)
    for kind in range(2):
        part = dot(left, hist_ref[kind].reshape(2 * TB * ORB, hist_ref.shape[-1]))

        @pl.when(k == 0)
        def _():
            acc_ref[kind] = part

        @pl.when(k > 0)
        def _():
            acc_ref[kind] += part

    @pl.when(block == current // TB)
    def _():
        at = current % TB
        real, imag = prop_ref[0], prop_ref[1]
        by_real = jnp.concatenate([real, imag], axis=0)
        by_imag = jnp.concatenate([-imag, real], axis=0)
        for kind in range(2):
            acc_ref[kind, : 2 * ORB] += dot(by_real, hist_ref[kind, 0, at]) + dot(
                by_imag, hist_ref[kind, 1, at]
            )

    @pl.when(block == (current + 1) // TB)
    def _():
        first = (current + 1) % TB * ORB
        pick = one_hot(iota((TB * ORB, 128), 0) == first + iota((TB * ORB, 128), 1) % ORB)
        tiled = dot(sigma_ref[1].reshape(2 * ORB, TB * ORB), pick)
        own = iota((2 * ORB, 128), 1) // ORB == iota((2 * ORB, 128), 0) % 4
        fold = one_hot(iota((DIAG, 2 * ORB), 1) // 4 == iota((DIAG, 2 * ORB), 0))
        diag_ref[...] = dot(fold, jnp.where(own, tiled, 0.0).astype(BF)) * 0.5

    @pl.when(k == pl.num_programs(0) - 1)
    def _():
        for kind in range(2):
            turned = acc_ref[kind].T.astype(BF)
            for blk in range(2):
                for part in range(16):
                    first = (blk * 16 + part) * 16
                    out_ref[kind * 16 + part, blk * 16 : blk * 16 + 16, :] = turned[first : first + 16]
        diag = diag_ref[...].astype(BF)
        for part in range(SLICES):
            out_ref[part, DATA:, :] = diag


def finish_kernel(in_ref, prop_ref, rows_ref, mirror_ref):
    sums = []
    for x in range(XS):
        total = in_ref[x, :DATA].astype(F32)
        for r in range(1, ROWS):
            total += in_ref[r * XS + x, :DATA].astype(F32)
        sums.append(total)
    total = jnp.concatenate(sums, axis=0)
    packed = in_ref[0, DATA:].astype(F32)
    for r in range(1, ROWS):
        packed += in_ref[r * XS, DATA:].astype(F32)
    lane = iota((ORB, 128), 1)
    left, right = lane < ORB, (lane >= ORB) & (lane < 2 * ORB)
    nothing = jnp.zeros((2 * ORB, 128), F32)

    def matrix(upper_left, upper_right, lower_left, lower_right):
        upper = jnp.where(left, upper_left, jnp.where(right, upper_right, 0.0))
        lower = jnp.where(left, lower_left, jnp.where(right, lower_right, 0.0))
        return jnp.concatenate([nothing, upper, lower], axis=0).astype(BF)

    tile = one_hot(iota((ORB, 128), 0) == iota((ORB, 128), 1) % ORB)
    real, imag = dot(prop_ref[0], tile), dot(prop_ref[1], tile)
    propagate = matrix(real, -imag, imag, real)
    spread = one_hot(iota((2 * ORB, DIAG), 0) // 4 == iota((2 * ORB, DIAG), 1))
    own = iota((2 * ORB, 128), 1) // ORB == iota((2 * ORB, 128), 0) % 4
    wide = jnp.where(own, dot(spread, packed.astype(BF)), 0.0).astype(BF)
    wrap = one_hot(iota((128, 128), 0) % ORB == iota((128, 128), 1) % ORB)
    diag = dot(wide, wrap)
    d_real, d_imag = diag[:ORB], diag[ORB:]
    turn = matrix(d_imag, d_real, -d_real, d_imag)
    low = total.astype(BF)
    new = (total + dot_nt(low, propagate) + dot_nt(low, turn)).astype(BF)
    rows_ref[...] = new
    size = XS * DATA
    lane_block = iota((size, 128), 1) // ORB
    place = iota((size, 128), 0) % 4
    signed = jnp.where(lane_block % 2 == 0, -new.astype(F32), new.astype(F32))
    result = jnp.where(lane_block == place, signed, 0.0)
    for d in range(1, 4):
        moved = jnp.where(lane_block == place, pltpu.roll(signed, 128 - ORB * d, 1), 0.0)
        result += jnp.where(
            place >= d, pltpu.roll(moved, d, 0), pltpu.roll(moved, size + d - 4, 0)
        )
    result = result.astype(BF)
    for z in range(ZS):
        mirror_ref[z] = result


def select_kernel(map_ref, blocks_ref, rows_ref, out_ref):
    for r in range(ROWS):
        for j in range(TB):
            block = map_ref[r * TB + j]
            column = block // 2
            start = pl.multiple_of(column // ZS * DATA + block % 2 * 16, 16)
            piece = blocks_ref[column % ZS, pl.ds(start, 16), :]
            for x in range(XS):
                out_ref[r * XS + x, j * 16 : j * 16 + 16, :] = piece
        for x in range(XS):
            out_ref[r * XS + x, 128:, :] = rows_ref[x * DATA : x * DATA + DATA, :]


def place_kernel(in_ref, rows_ref, mirror_ref, mixed_ref, tall_ref):
    for h in range(2):
        for pair in range(4):
            for half in range(2):
                j = pair * 2 + half
                for tm in range(TB):
                    mixed_ref[h, pair, pl.ds(half * 8 + tm, 16, stride=16), :] = in_ref[
                        tm * 2 + h, j * 16 : j * 16 + 16, :
                    ].astype(F32)
            for q in range(4):
                for g in range(4):
                    first = (q * 4 + g) * 16
                    mirror_ref[
                        g // 2, 0, g % 2, pair * 16 : pair * 16 + 16, (h * 4 + q) * 128 : (h * 4 + q) * 128 + 128
                    ] = mixed_ref[h, pair, first : first + 16, :].astype(BF)
    for blk in range(2):
        for part in range(16):
            first = (blk * 16 + part) * 16
            tall_ref[first : first + 16, :] = in_ref[part, 128 + blk * 16 : 144 + blk * 16, :].astype(F32)
    wide = tall_ref[...].T
    for g in range(4):
        rows_ref[g // 2, 0, g % 2] = wide[g * ORB : g * ORB + ORB, :]


def per_device(history, sigma_rows, propagator, block_map, step_index):
    smem = pl.BlockSpec(memory_space=pltpu.SMEM)
    vmem = pl.BlockSpec(memory_space=pltpu.VMEM)
    columns = history.shape[4]
    partial = pl.pallas_call(
        product_kernel,
        grid=(ROWS,),
        in_specs=[
            smem,
            smem,
            pl.BlockSpec((2, 2, TB, ORB, columns), lambda k: (0, 0, k, 0, 0)),
            pl.BlockSpec((2, 2, ORB, TB * ORB), lambda k: (0, 0, 0, k)),
            pl.BlockSpec((2, ORB, ORB), lambda k: (0, 0, 0)),
        ],
        out_specs=pl.BlockSpec((SLICES, DATA + DIAG, 128), lambda k: (0, 0, 0)),
        out_shape=jax.ShapeDtypeStruct((SLICES, DATA + DIAG, 128), BF),
        scratch_shapes=[pltpu.VMEM((2, 128, columns), F32), pltpu.VMEM((DIAG, 128), F32)],
        compiler_params=pltpu.CompilerParams(vmem_limit_bytes=24 << 20),
        name="products",
    )(block_map, step_index, history, sigma_rows, propagator)
    partial = lax.all_to_all(partial, ("row", "x"), 0, 0, tiled=True)
    new, copies = pl.pallas_call(
        finish_kernel,
        in_specs=[vmem, vmem],
        out_specs=[vmem, vmem],
        out_shape=[
            jax.ShapeDtypeStruct((XS * DATA, 128), BF),
            jax.ShapeDtypeStruct((ZS, XS * DATA, 128), BF),
        ],
        compiler_params=pltpu.CompilerParams(vmem_limit_bytes=24 << 20),
        name="finish",
    )(partial, propagator)
    blocks = lax.all_to_all(copies, "z", 0, 0, tiled=True)
    back = pl.pallas_call(
        select_kernel,
        in_specs=[smem, vmem, vmem],
        out_specs=vmem,
        out_shape=jax.ShapeDtypeStruct((SLICES, BACK, 128), BF),
        compiler_params=pltpu.CompilerParams(vmem_limit_bytes=24 << 20),
        name="select",
    )(block_map, blocks, new)
    back = lax.all_to_all(back, ("row", "x"), 0, 0, tiled=True)
    new_rows, mirror = pl.pallas_call(
        place_kernel,
        grid=(2,),
        in_specs=[pl.BlockSpec((SLICES // 2, BACK, 128), lambda kind: (kind, 0, 0))],
        out_specs=[
            pl.BlockSpec((2, 1, 2, ORB, columns), lambda kind: (0, kind, 0, 0, 0)),
            pl.BlockSpec((2, 1, 2, ROWS * TB, ORB * ORB), lambda kind: (0, kind, 0, 0, 0)),
        ],
        out_shape=[
            jax.ShapeDtypeStruct((2, 2, 2, ORB, columns), F32),
            jax.ShapeDtypeStruct((2, 2, 2, ROWS * TB, ORB * ORB), BF),
        ],
        scratch_shapes=[pltpu.VMEM((2, 4, 256, 128), F32), pltpu.VMEM((columns, 128), F32)],
        compiler_params=pltpu.CompilerParams(vmem_limit_bytes=24 << 20),
        name="place",
    )(back)
    return new_rows, mirror


def solution(mesh):
    split = Mesh(mesh.devices.reshape(ROWS, XS, ZS), ("row", "x", "z"))
    column = ("x", "z")
    return jax.shard_map(
        per_device,
        mesh=split,
        in_specs=(P(None, None, "row", None, column), P(None, None, None, "row"), P(), P(), P()),
        out_specs=(P(None, None, None, None, column), P(None, None, None, "row", None)),
        check_vma=False,
    )
```

```python
import jax
import jax.numpy as jnp
from jax import lax
from jax.experimental import pallas as pl
from jax.experimental.pallas import tpu as pltpu
from jax.sharding import Mesh, PartitionSpec as P

TB = 8
ORB = 32
ROWS = 8
XS = 4
YS = 4
PARTS = 16
ZS = 8
BF = jnp.bfloat16
F32 = jnp.float32
SLICES = ROWS * XS
DATA = 32
DIAG = 16
SPAN = 512
BACK = 160


def dot(a, b):
    return jnp.dot(a, b, preferred_element_type=F32)


def dot_nt(a, b):
    return lax.dot_general(a, b, (((1,), (1,)), ((), ())), preferred_element_type=F32)


def iota(shape, axis):
    return lax.broadcasted_iota(jnp.int32, shape, axis)


def one_hot(cond):
    return jnp.where(cond, 1.0, 0.0).astype(BF)


def product_kernel(
    step_ref, map_hbm, hist_hbm, sigma_hbm, prop_hbm, other_ref, own_ref,
    map_ref, hist_ref, sigma_ref, prop_ref, left_ref, acc_ref, hist_sem, sem,
):
    chunks = [
        pltpu.make_async_copy(
            hist_hbm.at[:, :, pl.ds(k * TB, TB)], hist_ref.at[k], hist_sem.at[k]
        )
        for k in range(ROWS)
    ]
    small = [
        pltpu.make_async_copy(source, target, sem.at[i])
        for i, (source, target) in enumerate(
            ((map_hbm, map_ref), (sigma_hbm, sigma_ref), (prop_hbm, prop_ref))
        )
    ]
    for copy in small:
        copy.start()
    for copy in chunks[:6]:
        copy.start()
    core = lax.axis_index("core")
    row = lax.axis_index("y") * 2 + core
    own_ref[SPAN:, :] = jnp.zeros((DIAG, 128), F32)
    other_ref[SPAN:, :] = jnp.zeros((DIAG, 128), BF)
    for copy in small:
        copy.wait()
    current = step_ref[0]
    offset = iota((1, TB * ORB), 1) // ORB
    blocks = [map_ref[row * ROWS + k] for k in range(ROWS)]
    for k in range(ROWS):
        times = blocks[k] * TB + offset
        beyond = times > current
        weight_two = jnp.where(beyond, 0.0, jnp.where(times == 0, 0.5, 1.0))
        weight_one = jnp.where(
            beyond, 0.0, jnp.where((times == 0) | (times == current), 0.5, 1.0)
        )
        lanes = slice(k * TB * ORB, (k + 1) * TB * ORB)
        for s, weight in enumerate((weight_one, weight_two)):
            real = (sigma_ref[s, 0, :, lanes].astype(F32) * weight).astype(BF)
            imag = (sigma_ref[s, 1, :, lanes].astype(F32) * weight).astype(BF)
            upper = slice(s * 2 * ORB, s * 2 * ORB + ORB)
            lower = slice(s * 2 * ORB + ORB, (s + 1) * 2 * ORB)
            left_ref[k, upper, : TB * ORB] = imag
            left_ref[k, lower, : TB * ORB] = -real
            left_ref[k, upper, TB * ORB :] = real
            left_ref[k, lower, TB * ORB :] = imag

    def holder(time):
        at = sum(jnp.where(blocks[k] == time // TB, k + 1, 0) for k in range(ROWS))
        return at > 0, jnp.maximum(at - 1, 0)

    holds_next, chunk_next = holder(current + 1)
    holds_now, chunk_now = holder(current)

    @pl.when(holds_next)
    def _():
        first = (current + 1) % TB * ORB
        lanes = pl.ds(pl.multiple_of(chunk_next * TB * ORB, TB * ORB), TB * ORB)
        pick = one_hot(iota((TB * ORB, 128), 0) == first + iota((TB * ORB, 128), 1) % ORB)
        tiled = dot(sigma_ref[1, :, :, lanes].reshape(2 * ORB, TB * ORB), pick)
        own = iota((2 * ORB, 128), 1) // ORB == iota((2 * ORB, 128), 0) % 4
        fold = one_hot(iota((DIAG, 2 * ORB), 1) // 4 == iota((DIAG, 2 * ORB), 0))
        diag = dot(fold, jnp.where(own, tiled, 0.0).astype(BF)) * 0.5
        own_ref[SPAN:, :] = diag
        other_ref[SPAN:, :] = diag.astype(BF)

    for k in range(ROWS):
        chunks[k].wait()
        if k + 6 < ROWS:
            chunks[k + 6].start()
        for kind in range(2):
            part = dot(left_ref[k], hist_ref[k, kind].reshape(2 * TB * ORB, hist_ref.shape[-1]))
            if k == 0:
                acc_ref[kind] = part
            else:
                acc_ref[kind] += part

    @pl.when(holds_now)
    def _():
        at = current % TB
        real, imag = prop_ref[0], prop_ref[1]
        by_real = jnp.concatenate([real, imag], axis=0)
        by_imag = jnp.concatenate([-imag, real], axis=0)
        for kind in range(2):
            acc_ref[kind, : 2 * ORB] += dot(by_real, hist_ref[chunk_now, kind, 0, at]) + dot(
                by_imag, hist_ref[chunk_now, kind, 1, at]
            )

    other_ref[:SPAN, :] = acc_ref[1 - core].T.astype(BF)
    own_ref[:SPAN, :] = acc_ref[core].T


def join_kernel(own_ref, other_ref, out_ref):
    total = (own_ref[...] + other_ref[...].astype(F32)).astype(BF)
    for part in range(PARTS):
        for blk in range(2):
            first = (blk * PARTS + part) * 16
            out_ref[part, blk * 16 : blk * 16 + 16, :] = total[first : first + 16]
        out_ref[part, DATA:, :] = total[SPAN:]


def finish_kernel(in_ref, prop_ref, rows_ref, mirror_ref):
    sums = []
    for x in range(XS):
        total = in_ref[x, :DATA].astype(F32)
        for r in range(1, YS):
            total += in_ref[r * XS + x, :DATA].astype(F32)
        sums.append(total)
    total = jnp.concatenate(sums, axis=0)
    packed = in_ref[0, DATA:].astype(F32)
    for r in range(1, YS):
        packed += in_ref[r * XS, DATA:].astype(F32)
    lane = iota((ORB, 128), 1)
    left, right = lane < ORB, (lane >= ORB) & (lane < 2 * ORB)
    nothing = jnp.zeros((2 * ORB, 128), F32)

    def matrix(upper_left, upper_right, lower_left, lower_right):
        upper = jnp.where(left, upper_left, jnp.where(right, upper_right, 0.0))
        lower = jnp.where(left, lower_left, jnp.where(right, lower_right, 0.0))
        return jnp.concatenate([nothing, upper, lower], axis=0).astype(BF)

    tile = one_hot(iota((ORB, 128), 0) == iota((ORB, 128), 1) % ORB)
    real, imag = dot(prop_ref[0], tile), dot(prop_ref[1], tile)
    propagate = matrix(real, -imag, imag, real)
    spread = one_hot(iota((2 * ORB, DIAG), 0) // 4 == iota((2 * ORB, DIAG), 1))
    own = iota((2 * ORB, 128), 1) // ORB == iota((2 * ORB, 128), 0) % 4
    wide = jnp.where(own, dot(spread, packed.astype(BF)), 0.0).astype(BF)
    wrap = one_hot(iota((128, 128), 0) % ORB == iota((128, 128), 1) % ORB)
    diag = dot(wide, wrap)
    d_real, d_imag = diag[:ORB], diag[ORB:]
    turn = matrix(d_imag, d_real, -d_real, d_imag)
    low = total.astype(BF)
    new = (total + dot_nt(low, propagate) + dot_nt(low, turn)).astype(BF)
    rows_ref[...] = new
    size = XS * DATA
    lane_block = iota((size, 128), 1) // ORB
    place = iota((size, 128), 0) % 4
    signed = jnp.where(lane_block % 2 == 0, -new.astype(F32), new.astype(F32))
    result = jnp.where(lane_block == place, signed, 0.0)
    for d in range(1, 4):
        moved = jnp.where(lane_block == place, pltpu.roll(signed, 128 - ORB * d, 1), 0.0)
        result += jnp.where(
            place >= d, pltpu.roll(moved, d, 0), pltpu.roll(moved, size + d - 4, 0)
        )
    result = result.astype(BF)
    for z in range(ZS):
        mirror_ref[z] = result


def select_kernel(map_ref, blocks_ref, rows_ref, out_ref):
    for r in range(ROWS):
        for j in range(TB):
            block = map_ref[r * TB + j]
            column = block // 2
            start = pl.multiple_of(column // ZS * DATA + block % 2 * 16, 16)
            piece = blocks_ref[column % ZS, pl.ds(start, 16), :]
            for x in range(XS):
                out_ref[r * XS + x, j * 16 : j * 16 + 16, :] = piece
        for x in range(XS):
            out_ref[r * XS + x, 128:, :] = rows_ref[x * DATA : x * DATA + DATA, :]


def place_kernel(in_ref, rows_ref, mirror_ref, mixed_ref, tall_ref):
    for h in range(2):
        for pair in range(4):
            for half in range(2):
                j = pair * 2 + half
                for tm in range(TB):
                    mixed_ref[h, pair, pl.ds(half * 8 + tm, 16, stride=16), :] = in_ref[
                        tm // 2, 0, tm % 2 * 2 + h, j * 16 : j * 16 + 16, :
                    ].astype(F32)
            for q in range(4):
                for g in range(4):
                    first = (q * 4 + g) * 16
                    mirror_ref[
                        g // 2, 0, g % 2, pair * 16 : pair * 16 + 16, (h * 4 + q) * 128 : (h * 4 + q) * 128 + 128
                    ] = mixed_ref[h, pair, first : first + 16, :].astype(BF)
    for blk in range(2):
        for part in range(16):
            first = (blk * 16 + part) * 16
            tall_ref[first : first + 16, :] = in_ref[
                part // XS, 0, part % XS, 128 + blk * 16 : 144 + blk * 16, :
            ].astype(F32)
    wide = tall_ref[...].T
    for g in range(4):
        rows_ref[g // 2, 0, g % 2] = wide[g * ORB : g * ORB + ORB, :]


def per_device(history, sigma_rows, propagator, block_map, step_index):
    smem = pl.BlockSpec(memory_space=pltpu.SMEM)
    vmem = pl.BlockSpec(memory_space=pltpu.VMEM)
    columns = history.shape[4]
    hbm = pl.BlockSpec(memory_space=pltpu.HBM)
    small = pltpu.CompilerParams(vmem_limit_bytes=16 << 20)
    inputs = (block_map, history, sigma_rows, propagator)
    other, own = pl.pallas_call(
        product_kernel,
        in_specs=[smem] + [hbm] * 4,
        out_specs=[vmem, vmem],
        out_shape=[
            jax.ShapeDtypeStruct((SPAN + DIAG, 128), BF),
            jax.ShapeDtypeStruct((SPAN + DIAG, 128), F32),
        ],
        scratch_shapes=[
            pltpu.SMEM(block_map.shape, jnp.int32),
            pltpu.VMEM((ROWS, 2, 2, TB, ORB, columns), BF),
            pltpu.VMEM(sigma_rows.shape, BF),
            pltpu.VMEM(propagator.shape, BF),
            pltpu.VMEM((ROWS, 128, 2 * TB * ORB), BF),
            pltpu.VMEM((2, 128, columns), F32),
            pltpu.SemaphoreType.DMA((ROWS,)),
            pltpu.SemaphoreType.DMA((3,)),
        ],
        compiler_params=pltpu.CompilerParams(vmem_limit_bytes=40 << 20),
        name="products",
    )(step_index, *(pltpu.with_memory_space_constraint(a, pltpu.HBM) for a in inputs))
    other = lax.ppermute(other, "core", ((0, 1), (1, 0)))
    partial = pl.pallas_call(
        join_kernel,
        in_specs=[vmem] * 2,
        out_specs=vmem,
        out_shape=jax.ShapeDtypeStruct((PARTS, DATA + DIAG, 128), BF),
        compiler_params=small,
        name="join",
    )(own, other)
    partial = lax.all_to_all(partial, ("y", "x"), 0, 0, tiled=True)
    new, copies = pl.pallas_call(
        finish_kernel,
        in_specs=[vmem, vmem],
        out_specs=[vmem, vmem],
        out_shape=[
            jax.ShapeDtypeStruct((XS * DATA, 128), BF),
            jax.ShapeDtypeStruct((ZS, XS * DATA, 128), BF),
        ],
        compiler_params=pltpu.CompilerParams(vmem_limit_bytes=16 << 20),
        name="finish",
    )(partial, propagator)
    blocks = lax.all_to_all(copies, "z", 0, 0, tiled=True)
    back = pl.pallas_call(
        select_kernel,
        in_specs=[smem, vmem, vmem],
        out_specs=vmem,
        out_shape=jax.ShapeDtypeStruct((SLICES, BACK, 128), BF),
        compiler_params=pltpu.CompilerParams(vmem_limit_bytes=16 << 20),
        name="select",
    )(block_map, blocks, new)
    back = lax.all_to_all(back, ("y", "core", "x"), 0, 0, tiled=True)
    back = back.reshape(YS, 2, XS, BACK, 128)
    new_rows, mirror = pl.pallas_call(
        place_kernel,
        grid=(2,),
        in_specs=[pl.BlockSpec((YS, 1, XS, BACK, 128), lambda kind: (0, kind, 0, 0, 0))],
        out_specs=[
            pl.BlockSpec((2, 1, 2, ORB, columns), lambda kind: (0, kind, 0, 0, 0)),
            pl.BlockSpec((2, 1, 2, ROWS * TB, ORB * ORB), lambda kind: (0, kind, 0, 0, 0)),
        ],
        out_shape=[
            jax.ShapeDtypeStruct((2, 2, 2, ORB, columns), F32),
            jax.ShapeDtypeStruct((2, 2, 2, ROWS * TB, ORB * ORB), BF),
        ],
        scratch_shapes=[pltpu.VMEM((2, 4, 256, 128), F32), pltpu.VMEM((columns, 128), F32)],
        compiler_params=pltpu.CompilerParams(vmem_limit_bytes=16 << 20),
        name="place",
    )(back)
    return new_rows, mirror


def solution(mesh):
    split = Mesh(mesh.devices.reshape(YS, 2, XS, ZS), ("y", "core", "x", "z"))
    row = ("y", "core")
    column = ("x", "z")
    return jax.shard_map(
        per_device,
        mesh=split,
        in_specs=(P(None, None, row, None, column), P(None, None, None, row), P(), P(), P()),
        out_specs=(P(None, None, None, None, column), P(None, None, None, row, None)),
        check_vma=False,
    )
```

```python
import jax
import jax.numpy as jnp
from jax import lax
from jax.experimental import pallas as pl
from jax.experimental.pallas import tpu as pltpu
from jax.sharding import Mesh, PartitionSpec as P

TB = 8
ORB = 32
ROWS = 8
XS = 4
YS = 4
PARTS = 16
ZS = 8
BF = jnp.bfloat16
F32 = jnp.float32
SLICES = ROWS * XS
DATA = 32
DIAG = 16
SPAN = 512
BACK = 160


def dot(a, b):
    return jnp.dot(a, b, preferred_element_type=F32)


def dot_nt(a, b):
    return lax.dot_general(a, b, (((1,), (1,)), ((), ())), preferred_element_type=F32)


def iota(shape, axis):
    return lax.broadcasted_iota(jnp.int32, shape, axis)


def one_hot(cond):
    return jnp.where(cond, 1.0, 0.0).astype(BF)


def product_kernel(
    step_ref, map_hbm, hist_hbm, sigma_hbm, prop_hbm, other_ref, own_ref, map_ref,
    hist_ref, sigma_ref, prop_ref, left_ref, acc_ref, hist_sem, sem,
):
    chunks = [
        pltpu.make_async_copy(
            hist_hbm.at[:, :, pl.ds(k * TB, TB)], hist_ref.at[k], hist_sem.at[k]
        )
        for k in range(ROWS)
    ]
    small = [
        pltpu.make_async_copy(source, target, sem.at[i])
        for i, (source, target) in enumerate(
            ((map_hbm, map_ref), (sigma_hbm, sigma_ref), (prop_hbm, prop_ref))
        )
    ]
    for copy in small:
        copy.start()
    for copy in chunks[:6]:
        copy.start()
    core = lax.axis_index("core")
    row = lax.axis_index("y") * 2 + core
    own_ref[SPAN:, :] = jnp.zeros((DIAG, 128), F32)
    other_ref[SPAN:, :] = jnp.zeros((DIAG, 128), BF)
    for copy in small:
        copy.wait()
    current = step_ref[0]
    offset = iota((1, TB * ORB), 1) // ORB
    blocks = [map_ref[row * ROWS + k] for k in range(ROWS)]
    for k in range(ROWS):
        times = blocks[k] * TB + offset
        beyond = times > current
        weight_two = jnp.where(beyond, 0.0, jnp.where(times == 0, 0.5, 1.0))
        weight_one = jnp.where(
            beyond, 0.0, jnp.where((times == 0) | (times == current), 0.5, 1.0)
        )
        lanes = slice(k * TB * ORB, (k + 1) * TB * ORB)
        for s, weight in enumerate((weight_one, weight_two)):
            real = (sigma_ref[s, 0, :, lanes].astype(F32) * weight).astype(BF)
            imag = (sigma_ref[s, 1, :, lanes].astype(F32) * weight).astype(BF)
            upper = slice(s * 2 * ORB, s * 2 * ORB + ORB)
            lower = slice(s * 2 * ORB + ORB, (s + 1) * 2 * ORB)
            left_ref[k, upper, : TB * ORB] = imag
            left_ref[k, lower, : TB * ORB] = -real
            left_ref[k, upper, TB * ORB :] = real
            left_ref[k, lower, TB * ORB :] = imag

    def holder(time):
        at = sum(jnp.where(blocks[k] == time // TB, k + 1, 0) for k in range(ROWS))
        return at > 0, jnp.maximum(at - 1, 0)

    holds_next, chunk_next = holder(current + 1)
    holds_now, chunk_now = holder(current)

    @pl.when(holds_next)
    def _():
        first = (current + 1) % TB * ORB
        lanes = pl.ds(pl.multiple_of(chunk_next * TB * ORB, TB * ORB), TB * ORB)
        pick = one_hot(iota((TB * ORB, 128), 0) == first + iota((TB * ORB, 128), 1) % ORB)
        tiled = dot(sigma_ref[1, :, :, lanes].reshape(2 * ORB, TB * ORB), pick)
        own = iota((2 * ORB, 128), 1) // ORB == iota((2 * ORB, 128), 0) % 4
        fold = one_hot(iota((DIAG, 2 * ORB), 1) // 4 == iota((DIAG, 2 * ORB), 0))
        diag = dot(fold, jnp.where(own, tiled, 0.0).astype(BF)) * 0.5
        own_ref[SPAN:, :] = diag
        other_ref[SPAN:, :] = diag.astype(BF)

    for k in range(ROWS):
        chunks[k].wait()
        if k + 6 < ROWS:
            chunks[k + 6].start()
        for kind in range(2):
            part = dot(left_ref[k], hist_ref[k, kind].reshape(2 * TB * ORB, hist_ref.shape[-1]))
            if k == 0:
                acc_ref[kind] = part
            else:
                acc_ref[kind] += part

    @pl.when(holds_now)
    def _():
        at = current % TB
        real, imag = prop_ref[0], prop_ref[1]
        by_real = jnp.concatenate([real, imag], axis=0)
        by_imag = jnp.concatenate([-imag, real], axis=0)
        for kind in range(2):
            acc_ref[kind, : 2 * ORB] += dot(by_real, hist_ref[chunk_now, kind, 0, at]) + dot(
                by_imag, hist_ref[chunk_now, kind, 1, at]
            )

    other_ref[:SPAN, :] = acc_ref[1 - core].T.astype(BF)
    own_ref[:SPAN, :] = acc_ref[core].T


def join_kernel(own_ref, other_ref, out_ref):
    total = (own_ref[...] + other_ref[...].astype(F32)).astype(BF)
    for part in range(PARTS):
        for blk in range(2):
            first = (blk * PARTS + part) * 16
            out_ref[part, blk * 16 : blk * 16 + 16, :] = total[first : first + 16]
        out_ref[part, DATA:, :] = total[SPAN:]


def finish_kernel(in_ref, prop_ref, rows_ref, mirror_ref):
    sums = []
    for x in range(XS):
        total = in_ref[x, :DATA].astype(F32)
        for r in range(1, YS):
            total += in_ref[r * XS + x, :DATA].astype(F32)
        sums.append(total)
    total = jnp.concatenate(sums, axis=0)
    packed = in_ref[0, DATA:].astype(F32)
    for r in range(1, YS):
        packed += in_ref[r * XS, DATA:].astype(F32)
    lane = iota((ORB, 128), 1)
    left, right = lane < ORB, (lane >= ORB) & (lane < 2 * ORB)
    nothing = jnp.zeros((2 * ORB, 128), F32)

    def matrix(upper_left, upper_right, lower_left, lower_right):
        upper = jnp.where(left, upper_left, jnp.where(right, upper_right, 0.0))
        lower = jnp.where(left, lower_left, jnp.where(right, lower_right, 0.0))
        return jnp.concatenate([nothing, upper, lower], axis=0).astype(BF)

    tile = one_hot(iota((ORB, 128), 0) == iota((ORB, 128), 1) % ORB)
    real, imag = dot(prop_ref[0], tile), dot(prop_ref[1], tile)
    propagate = matrix(real, -imag, imag, real)
    spread = one_hot(iota((2 * ORB, DIAG), 0) // 4 == iota((2 * ORB, DIAG), 1))
    own = iota((2 * ORB, 128), 1) // ORB == iota((2 * ORB, 128), 0) % 4
    wide = jnp.where(own, dot(spread, packed.astype(BF)), 0.0).astype(BF)
    wrap = one_hot(iota((128, 128), 0) % ORB == iota((128, 128), 1) % ORB)
    diag = dot(wide, wrap)
    d_real, d_imag = diag[:ORB], diag[ORB:]
    turn = matrix(d_imag, d_real, -d_real, d_imag)
    low = total.astype(BF)
    new = (total + dot_nt(low, propagate) + dot_nt(low, turn)).astype(BF)
    rows_ref[...] = new
    size = XS * DATA
    lane_block = iota((size, 128), 1) // ORB
    place = iota((size, 128), 0) % 4
    signed = jnp.where(lane_block % 2 == 0, -new.astype(F32), new.astype(F32))
    result = jnp.where(lane_block == place, signed, 0.0)
    for d in range(1, 4):
        moved = jnp.where(lane_block == place, pltpu.roll(signed, 128 - ORB * d, 1), 0.0)
        result += jnp.where(
            place >= d, pltpu.roll(moved, d, 0), pltpu.roll(moved, size + d - 4, 0)
        )
    result = result.astype(BF)
    for z in range(ZS):
        mirror_ref[z] = result


def select_kernel(map_ref, blocks_ref, rows_ref, out_ref):
    for r in range(ROWS):
        for j in range(TB):
            block = map_ref[r * TB + j]
            column = block // 2
            start = pl.multiple_of(column // ZS * DATA + block % 2 * 16, 16)
            piece = blocks_ref[column % ZS, pl.ds(start, 16), :]
            for x in range(XS):
                out_ref[r * XS + x, j * 16 : j * 16 + 16, :] = piece
        for x in range(XS):
            out_ref[r * XS + x, 128:, :] = rows_ref[x * DATA : x * DATA + DATA, :]


def place_kernel(in_ref, rows_hbm, mirror_hbm, mixed_ref, tall_ref, rows_ref, mirror_ref, rows_sem, mirror_sem):
    copies = []

    def send(source, target, semaphore):
        copies.append(pltpu.make_async_copy(source, target, semaphore))
        copies[-1].start()

    for kind in range(2):
        for blk in range(2):
            for part in range(PARTS):
                first = (blk * PARTS + part) * 16
                tall_ref[kind, first : first + 16, :] = in_ref[
                    part // XS, kind, part % XS, 128 + blk * 16 : 144 + blk * 16, :
                ].astype(F32)
        wide = tall_ref[kind].T
        for g in range(4):
            rows_ref[g // 2, kind, g % 2] = wide[g * ORB : g * ORB + ORB, :]
        send(rows_ref.at[:, kind], rows_hbm.at[:, kind], rows_sem.at[kind])
    for kind in range(2):
        for pair in range(4):
            for h in range(2):
                for half in range(2):
                    j = pair * 2 + half
                    for tm in range(TB):
                        mixed_ref[kind, h, pair, pl.ds(half * 8 + tm, 16, stride=16), :] = in_ref[
                            tm // 2, kind, tm % 2 * 2 + h, j * 16 : j * 16 + 16, :
                        ].astype(F32)
                for q in range(4):
                    for g in range(4):
                        first = (q * 4 + g) * 16
                        lanes = slice((h * 4 + q) * 128, (h * 4 + q) * 128 + 128)
                        mirror_ref[g // 2, kind, g % 2, pair * 16 : pair * 16 + 16, lanes] = mixed_ref[
                            kind, h, pair, first : first + 16, :
                        ].astype(BF)
            own = (slice(None), kind, slice(None), pl.ds(pair * 16, 16))
            send(mirror_ref.at[own], mirror_hbm.at[own], mirror_sem.at[kind, pair])
    for copy in copies:
        copy.wait()


def per_device(history, sigma_rows, propagator, block_map, step_index):
    smem = pl.BlockSpec(memory_space=pltpu.SMEM)
    vmem = pl.BlockSpec(memory_space=pltpu.VMEM)
    columns = history.shape[4]
    hbm = pl.BlockSpec(memory_space=pltpu.HBM)
    small = pltpu.CompilerParams(vmem_limit_bytes=16 << 20)
    inputs = (block_map, history, sigma_rows, propagator)
    other, own, kept_map = pl.pallas_call(
        product_kernel,
        in_specs=[smem] + [hbm] * 4,
        out_specs=[vmem, vmem, smem],
        out_shape=[
            jax.ShapeDtypeStruct((SPAN + DIAG, 128), BF),
            jax.ShapeDtypeStruct((SPAN + DIAG, 128), F32),
            pltpu.SMEM(block_map.shape, jnp.int32),
        ],
        scratch_shapes=[
            pltpu.VMEM((ROWS, 2, 2, TB, ORB, columns), BF),
            pltpu.VMEM(sigma_rows.shape, BF),
            pltpu.VMEM(propagator.shape, BF),
            pltpu.VMEM((ROWS, 128, 2 * TB * ORB), BF),
            pltpu.VMEM((2, 128, columns), F32),
            pltpu.SemaphoreType.DMA((ROWS,)),
            pltpu.SemaphoreType.DMA((3,)),
        ],
        compiler_params=pltpu.CompilerParams(vmem_limit_bytes=40 << 20),
        name="products",
    )(step_index, *(pltpu.with_memory_space_constraint(a, pltpu.HBM) for a in inputs))
    other = lax.ppermute(other, "core", ((0, 1), (1, 0)))
    partial = pl.pallas_call(
        join_kernel,
        in_specs=[vmem] * 2,
        out_specs=vmem,
        out_shape=jax.ShapeDtypeStruct((PARTS, DATA + DIAG, 128), BF),
        compiler_params=small,
        name="join",
    )(own, other)
    partial = lax.all_to_all(partial, ("y", "x"), 0, 0, tiled=True)
    new, copies = pl.pallas_call(
        finish_kernel,
        in_specs=[vmem, vmem],
        out_specs=[vmem, vmem],
        out_shape=[
            jax.ShapeDtypeStruct((XS * DATA, 128), BF),
            jax.ShapeDtypeStruct((ZS, XS * DATA, 128), BF),
        ],
        compiler_params=pltpu.CompilerParams(vmem_limit_bytes=16 << 20),
        name="finish",
    )(partial, propagator)
    blocks = lax.all_to_all(copies, "z", 0, 0, tiled=True)
    back = pl.pallas_call(
        select_kernel,
        in_specs=[smem, vmem, vmem],
        out_specs=vmem,
        out_shape=jax.ShapeDtypeStruct((SLICES, BACK, 128), BF),
        compiler_params=pltpu.CompilerParams(vmem_limit_bytes=16 << 20),
        name="select",
    )(kept_map, blocks, new)
    back = lax.all_to_all(back, ("y", "core", "x"), 0, 0, tiled=True)
    back = back.reshape(YS, 2, XS, BACK, 128)
    rows_shape = (2, 2, 2, ORB, columns)
    mirror_shape = (2, 2, 2, ROWS * TB, ORB * ORB)
    new_rows, mirror = pl.pallas_call(
        place_kernel,
        in_specs=[vmem],
        out_specs=[pl.BlockSpec(memory_space=pl.ANY)] * 2,
        out_shape=[jax.ShapeDtypeStruct(rows_shape, F32), jax.ShapeDtypeStruct(mirror_shape, BF)],
        scratch_shapes=[
            pltpu.VMEM((2, 2, 4, 256, 128), F32),
            pltpu.VMEM((2, columns, 128), F32),
            pltpu.VMEM(rows_shape, F32),
            pltpu.VMEM(mirror_shape, BF),
            pltpu.SemaphoreType.DMA((2,)),
            pltpu.SemaphoreType.DMA((2, 4)),
        ],
        compiler_params=small,
        name="place",
    )(back)
    return new_rows, mirror


def solution(mesh):
    split = Mesh(mesh.devices.reshape(YS, 2, XS, ZS), ("y", "core", "x", "z"))
    row = ("y", "core")
    column = ("x", "z")
    return jax.shard_map(
        per_device,
        mesh=split,
        in_specs=(P(None, None, row, None, column), P(None, None, None, row), P(), P(), P()),
        out_specs=(P(None, None, None, None, column), P(None, None, None, row, None)),
        check_vma=False,
    )
```

```python
import jax
import jax.numpy as jnp
from jax import lax
from jax.experimental import pallas as pl
from jax.experimental.pallas import tpu as pltpu
from jax.sharding import Mesh, PartitionSpec as P

TB = 8
ORB = 32
ROWS = 8
XS = 4
YS = 4
PARTS = 16
ZS = 8
BF = jnp.bfloat16
F32 = jnp.float32
SLICES = ROWS * XS
DATA = 32
DIAG = 16
SPAN = 512
BACK = 160


def dot(a, b):
    return jnp.dot(a, b, preferred_element_type=F32)


def dot_nt(a, b):
    return lax.dot_general(a, b, (((1,), (1,)), ((), ())), preferred_element_type=F32)


def iota(shape, axis):
    return lax.broadcasted_iota(jnp.int32, shape, axis)


def one_hot(cond):
    return jnp.where(cond, 1.0, 0.0).astype(BF)


def product_kernel(
    step_ref, map_hbm, hist_hbm, sigma_hbm, prop_hbm, other_ref, own_ref, map_ref,
    hist_ref, sigma_ref, prop_ref, left_ref, acc_ref, hist_sem, sem,
):
    chunks = [
        pltpu.make_async_copy(
            hist_hbm.at[:, :, pl.ds(k * TB, TB)], hist_ref.at[k], hist_sem.at[k]
        )
        for k in range(ROWS)
    ]
    small = [
        pltpu.make_async_copy(source, target, sem.at[i])
        for i, (source, target) in enumerate(
            ((map_hbm, map_ref), (sigma_hbm, sigma_ref), (prop_hbm, prop_ref))
        )
    ]
    for copy in small:
        copy.start()
    for copy in chunks[:6]:
        copy.start()
    core = lax.axis_index("core")
    row = lax.axis_index("y") * 2 + core
    own_ref[SPAN:, :] = jnp.zeros((DIAG, 128), F32)
    other_ref[SPAN:, :] = jnp.zeros((DIAG, 128), BF)
    for copy in small:
        copy.wait()
    current = step_ref[0]
    offset = iota((1, TB * ORB), 1) // ORB
    blocks = [map_ref[row * ROWS + k] for k in range(ROWS)]
    for k in range(ROWS):
        times = blocks[k] * TB + offset
        beyond = times > current
        weight_two = jnp.where(beyond, 0.0, jnp.where(times == 0, 0.5, 1.0))
        weight_one = jnp.where(
            beyond, 0.0, jnp.where((times == 0) | (times == current), 0.5, 1.0)
        )
        lanes = slice(k * TB * ORB, (k + 1) * TB * ORB)
        for s, weight in enumerate((weight_one, weight_two)):
            real = (sigma_ref[s, 0, :, lanes].astype(F32) * weight).astype(BF)
            imag = (sigma_ref[s, 1, :, lanes].astype(F32) * weight).astype(BF)
            upper = slice(s * 2 * ORB, s * 2 * ORB + ORB)
            lower = slice(s * 2 * ORB + ORB, (s + 1) * 2 * ORB)
            left_ref[k, upper, : TB * ORB] = imag
            left_ref[k, lower, : TB * ORB] = -real
            left_ref[k, upper, TB * ORB :] = real
            left_ref[k, lower, TB * ORB :] = imag

    def holder(time):
        at = sum(jnp.where(blocks[k] == time // TB, k + 1, 0) for k in range(ROWS))
        return at > 0, jnp.maximum(at - 1, 0)

    holds_next, chunk_next = holder(current + 1)
    holds_now, chunk_now = holder(current)

    @pl.when(holds_next)
    def _():
        first = (current + 1) % TB * ORB
        lanes = pl.ds(pl.multiple_of(chunk_next * TB * ORB, TB * ORB), TB * ORB)
        pick = one_hot(iota((TB * ORB, 128), 0) == first + iota((TB * ORB, 128), 1) % ORB)
        tiled = dot(sigma_ref[1, :, :, lanes].reshape(2 * ORB, TB * ORB), pick)
        own = iota((2 * ORB, 128), 1) // ORB == iota((2 * ORB, 128), 0) % 4
        fold = one_hot(iota((DIAG, 2 * ORB), 1) // 4 == iota((DIAG, 2 * ORB), 0))
        diag = dot(fold, jnp.where(own, tiled, 0.0).astype(BF)) * 0.5
        own_ref[SPAN:, :] = diag
        other_ref[SPAN:, :] = diag.astype(BF)

    for k in range(ROWS):
        chunks[k].wait()
        if k + 6 < ROWS:
            chunks[k + 6].start()
        for kind in range(2):
            part = dot(left_ref[k], hist_ref[k, kind].reshape(2 * TB * ORB, hist_ref.shape[-1]))
            if k == 0:
                acc_ref[kind] = part
            else:
                acc_ref[kind] += part

    @pl.when(holds_now)
    def _():
        at = current % TB
        real, imag = prop_ref[0], prop_ref[1]
        by_real = jnp.concatenate([real, imag], axis=0)
        by_imag = jnp.concatenate([-imag, real], axis=0)
        for kind in range(2):
            acc_ref[kind, : 2 * ORB] += dot(by_real, hist_ref[chunk_now, kind, 0, at]) + dot(
                by_imag, hist_ref[chunk_now, kind, 1, at]
            )

    other_ref[:SPAN, :] = acc_ref[1 - core].T.astype(BF)
    own_ref[:SPAN, :] = acc_ref[core].T


def join_kernel(own_ref, other_ref, out_ref):
    total = (own_ref[...] + other_ref[...].astype(F32)).astype(BF)
    for part in range(PARTS):
        for blk in range(2):
            first = (blk * PARTS + part) * 16
            out_ref[part, blk * 16 : blk * 16 + 16, :] = total[first : first + 16]
        out_ref[part, DATA:, :] = total[SPAN:]


def finish_kernel(in_ref, prop_ref, rows_ref, mirror_ref):
    sums = []
    for x in range(XS):
        total = in_ref[x, :DATA].astype(F32)
        for r in range(1, YS):
            total += in_ref[r * XS + x, :DATA].astype(F32)
        sums.append(total)
    total = jnp.concatenate(sums, axis=0)
    packed = in_ref[0, DATA:].astype(F32)
    for r in range(1, YS):
        packed += in_ref[r * XS, DATA:].astype(F32)
    lane = iota((ORB, 128), 1)
    left, right = lane < ORB, (lane >= ORB) & (lane < 2 * ORB)
    nothing = jnp.zeros((2 * ORB, 128), F32)

    def matrix(upper_left, upper_right, lower_left, lower_right):
        upper = jnp.where(left, upper_left, jnp.where(right, upper_right, 0.0))
        lower = jnp.where(left, lower_left, jnp.where(right, lower_right, 0.0))
        return jnp.concatenate([nothing, upper, lower], axis=0).astype(BF)

    tile = one_hot(iota((ORB, 128), 0) == iota((ORB, 128), 1) % ORB)
    real, imag = dot(prop_ref[0], tile), dot(prop_ref[1], tile)
    propagate = matrix(real, -imag, imag, real)
    spread = one_hot(iota((2 * ORB, DIAG), 0) // 4 == iota((2 * ORB, DIAG), 1))
    own = iota((2 * ORB, 128), 1) // ORB == iota((2 * ORB, 128), 0) % 4
    wide = jnp.where(own, dot(spread, packed.astype(BF)), 0.0).astype(BF)
    wrap = one_hot(iota((128, 128), 0) % ORB == iota((128, 128), 1) % ORB)
    diag = dot(wide, wrap)
    d_real, d_imag = diag[:ORB], diag[ORB:]
    turn = matrix(d_imag, d_real, -d_real, d_imag)
    low = total.astype(BF)
    new = (total + dot_nt(low, propagate) + dot_nt(low, turn)).astype(BF)
    rows_ref[...] = new
    size = XS * DATA
    lane_block = iota((size, 128), 1) // ORB
    place = iota((size, 128), 0) % 4
    signed = jnp.where(lane_block % 2 == 0, -new.astype(F32), new.astype(F32))
    result = jnp.where(lane_block == place, signed, 0.0)
    for d in range(1, 4):
        moved = jnp.where(lane_block == place, pltpu.roll(signed, 128 - ORB * d, 1), 0.0)
        result += jnp.where(
            place >= d, pltpu.roll(moved, d, 0), pltpu.roll(moved, size + d - 4, 0)
        )
    result = result.astype(BF)
    for z in range(ZS):
        mirror_ref[z] = result


def select_kernel(map_ref, blocks_ref, rows_ref, out_ref):
    for r in range(ROWS):
        for j in range(TB):
            block = map_ref[r * TB + j]
            column = block // 2
            start = pl.multiple_of(column // ZS * DATA + block % 2 * 16, 16)
            piece = blocks_ref[column % ZS, pl.ds(start, 16), :]
            for x in range(XS):
                out_ref[r * XS + x, j * 16 : j * 16 + 16, :] = piece
        for x in range(XS):
            out_ref[r * XS + x, 128:, :] = rows_ref[x * DATA : x * DATA + DATA, :]


def place_kernel(in_ref, rows_hbm, mirror_hbm, mixed_ref, tall_ref, rows_ref, mirror_ref, rows_sem, mirror_sem):
    copies = []

    def send(source, target, semaphore):
        copies.append(pltpu.make_async_copy(source, target, semaphore))
        copies[-1].start()

    for kind in range(2):
        for blk in range(2):
            for part in range(PARTS):
                first = (blk * PARTS + part) * 16
                tall_ref[kind, first : first + 16, :] = in_ref[
                    part // XS, kind, part % XS, 128 + blk * 16 : 144 + blk * 16, :
                ].astype(F32)
        wide = tall_ref[kind].T
        for g in range(4):
            rows_ref[g // 2, kind, g % 2] = wide[g * ORB : g * ORB + ORB, :]
        send(rows_ref.at[:, kind], rows_hbm.at[:, kind], rows_sem.at[kind])
    for kind in range(2):
        for pair in range(4):
            for h in range(2):
                for half in range(2):
                    j = pair * 2 + half
                    for tm in range(TB):
                        mixed_ref[kind, h, pair, pl.ds(half * 8 + tm, 16, stride=16), :] = in_ref[
                            tm // 2, kind, tm % 2 * 2 + h, j * 16 : j * 16 + 16, :
                        ].astype(F32)
                for q in range(4):
                    for g in range(4):
                        first = (q * 4 + g) * 16
                        lanes = slice((h * 4 + q) * 128, (h * 4 + q) * 128 + 128)
                        mirror_ref[g // 2, kind, g % 2, pair * 16 : pair * 16 + 16, lanes] = mixed_ref[
                            kind, h, pair, first : first + 16, :
                        ].astype(BF)
            own = (slice(None), kind, slice(None), pl.ds(pair * 16, 16))
            send(mirror_ref.at[own], mirror_hbm.at[own], mirror_sem.at[kind, pair])
    for copy in copies:
        copy.wait()


def per_device(history, sigma_rows, propagator, block_map, step_index):
    smem = pl.BlockSpec(memory_space=pltpu.SMEM)
    vmem = pl.BlockSpec(memory_space=pltpu.VMEM)
    columns = history.shape[4]
    hbm = pl.BlockSpec(memory_space=pltpu.HBM)
    small = pltpu.CompilerParams(vmem_limit_bytes=16 << 20)
    inputs = (block_map, history, sigma_rows, propagator)
    other, own, kept_map = pl.pallas_call(
        product_kernel,
        in_specs=[smem] + [hbm] * 4,
        out_specs=[vmem, vmem, smem],
        out_shape=[
            jax.ShapeDtypeStruct((SPAN + DIAG, 128), BF),
            jax.ShapeDtypeStruct((SPAN + DIAG, 128), F32),
            pltpu.SMEM(block_map.shape, jnp.int32),
        ],
        scratch_shapes=[
            pltpu.VMEM((ROWS, 2, 2, TB, ORB, columns), BF),
            pltpu.VMEM(sigma_rows.shape, BF),
            pltpu.VMEM(propagator.shape, BF),
            pltpu.VMEM((ROWS, 128, 2 * TB * ORB), BF),
            pltpu.VMEM((2, 128, columns), F32),
            pltpu.SemaphoreType.DMA((ROWS,)),
            pltpu.SemaphoreType.DMA((3,)),
        ],
        compiler_params=pltpu.CompilerParams(vmem_limit_bytes=40 << 20),
        name="products",
    )(step_index, *(pltpu.with_memory_space_constraint(a, pltpu.HBM) for a in inputs))
    other = lax.ppermute(other, "core", ((0, 1), (1, 0)))
    partial = pl.pallas_call(
        join_kernel,
        in_specs=[vmem] * 2,
        out_specs=vmem,
        out_shape=jax.ShapeDtypeStruct((PARTS, DATA + DIAG, 128), BF),
        compiler_params=small,
        name="join",
    )(own, other)
    partial = lax.all_to_all(partial, ("y", "x"), 0, 0, tiled=True)
    new, copies = pl.pallas_call(
        finish_kernel,
        in_specs=[vmem, vmem],
        out_specs=[vmem, vmem],
        out_shape=[
            jax.ShapeDtypeStruct((XS * DATA, 128), BF),
            jax.ShapeDtypeStruct((ZS, XS * DATA, 128), BF),
        ],
        compiler_params=pltpu.CompilerParams(vmem_limit_bytes=16 << 20),
        name="finish",
    )(partial, propagator)
    blocks = lax.all_to_all(copies, "z", 0, 0, tiled=True)
    back = pl.pallas_call(
        select_kernel,
        in_specs=[smem, vmem, vmem],
        out_specs=vmem,
        out_shape=jax.ShapeDtypeStruct((SLICES, BACK, 128), BF),
        compiler_params=pltpu.CompilerParams(vmem_limit_bytes=16 << 20),
        name="select",
    )(kept_map, blocks, new)
    back = lax.all_to_all(back, ("y", "core", "x"), 0, 0, tiled=True)
    back = back.reshape(YS, 2, XS, BACK, 128)
    rows_shape = (2, 2, 2, ORB, columns)
    mirror_shape = (2, 2, 2, ROWS * TB, ORB * ORB)
    new_rows, mirror = pl.pallas_call(
        place_kernel,
        in_specs=[vmem],
        out_specs=[pl.BlockSpec(memory_space=pl.ANY)] * 2,
        out_shape=[jax.ShapeDtypeStruct(rows_shape, F32), jax.ShapeDtypeStruct(mirror_shape, BF)],
        scratch_shapes=[
            pltpu.VMEM((2, 2, 4, 272, 128), F32),
            pltpu.VMEM((2, columns, 128), F32),
            pltpu.VMEM(rows_shape, F32),
            pltpu.VMEM(mirror_shape, BF),
            pltpu.SemaphoreType.DMA((2,)),
            pltpu.SemaphoreType.DMA((2, 4)),
        ],
        compiler_params=small,
        name="place",
    )(back)
    return new_rows, mirror


def solution(mesh):
    split = Mesh(mesh.devices.reshape(YS, 2, XS, ZS), ("y", "core", "x", "z"))
    row = ("y", "core")
    column = ("x", "z")
    return jax.shard_map(
        per_device,
        mesh=split,
        in_specs=(P(None, None, row, None, column), P(None, None, None, row), P(), P(), P()),
        out_specs=(P(None, None, None, None, column), P(None, None, None, row, None)),
        check_vma=False,
    )
```

```python
import jax
import jax.numpy as jnp
from jax import lax
from jax.experimental import pallas as pl
from jax.experimental.pallas import tpu as pltpu
from jax.sharding import Mesh, PartitionSpec as P

TB = 8
ORB = 32
ROWS = 8
XS = 4
YS = 4
PARTS = 16
ZS = 8
BF = jnp.bfloat16
F32 = jnp.float32
SLICES = ROWS * XS
DATA = 32
DIAG = 16
SPAN = 512
BACK = 160


def dot(a, b):
    return jnp.dot(a, b, preferred_element_type=F32)


def dot_nt(a, b):
    return lax.dot_general(a, b, (((1,), (1,)), ((), ())), preferred_element_type=F32)


def iota(shape, axis):
    return lax.broadcasted_iota(jnp.int32, shape, axis)


def one_hot(cond):
    return jnp.where(cond, 1.0, 0.0).astype(BF)


def product_kernel(
    step_ref, map_hbm, hist_hbm, sigma_hbm, prop_hbm, other_ref, own_ref, map_ref,
    hist_ref, sigma_ref, prop_ref, left_ref, acc_ref, hist_sem, sem,
):
    chunks = [
        pltpu.make_async_copy(
            hist_hbm.at[:, :, pl.ds(k * TB, TB)], hist_ref.at[k], hist_sem.at[k]
        )
        for k in range(ROWS)
    ]
    small = [
        pltpu.make_async_copy(source, target, sem.at[i])
        for i, (source, target) in enumerate(
            ((map_hbm, map_ref), (sigma_hbm, sigma_ref), (prop_hbm, prop_ref))
        )
    ]
    for copy in small:
        copy.start()
    for copy in chunks[:6]:
        copy.start()
    core = lax.axis_index("core")
    row = lax.axis_index("y") * 2 + core
    own_ref[SPAN:, :] = jnp.zeros((DIAG, 128), F32)
    other_ref[SPAN:, :] = jnp.zeros((DIAG, 128), BF)
    for copy in small:
        copy.wait()
    current = step_ref[0]
    offset = iota((1, TB * ORB), 1) // ORB
    blocks = [map_ref[row * ROWS + k] for k in range(ROWS)]
    for k in range(ROWS):
        times = blocks[k] * TB + offset
        beyond = times > current
        weight_two = jnp.where(beyond, 0.0, jnp.where(times == 0, 0.5, 1.0))
        weight_one = jnp.where(
            beyond, 0.0, jnp.where((times == 0) | (times == current), 0.5, 1.0)
        )
        lanes = slice(k * TB * ORB, (k + 1) * TB * ORB)
        for s, weight in enumerate((weight_one, weight_two)):
            real = (sigma_ref[s, 0, :, lanes].astype(F32) * weight).astype(BF)
            imag = (sigma_ref[s, 1, :, lanes].astype(F32) * weight).astype(BF)
            upper = slice(s * 2 * ORB, s * 2 * ORB + ORB)
            lower = slice(s * 2 * ORB + ORB, (s + 1) * 2 * ORB)
            left_ref[k, upper, : TB * ORB] = imag
            left_ref[k, lower, : TB * ORB] = -real
            left_ref[k, upper, TB * ORB :] = real
            left_ref[k, lower, TB * ORB :] = imag

    def holder(time):
        at = sum(jnp.where(blocks[k] == time // TB, k + 1, 0) for k in range(ROWS))
        return at > 0, jnp.maximum(at - 1, 0)

    holds_next, chunk_next = holder(current + 1)
    holds_now, chunk_now = holder(current)

    @pl.when(holds_next)
    def _():
        first = (current + 1) % TB * ORB
        lanes = pl.ds(pl.multiple_of(chunk_next * TB * ORB, TB * ORB), TB * ORB)
        pick = one_hot(iota((TB * ORB, 128), 0) == first + iota((TB * ORB, 128), 1) % ORB)
        tiled = dot(sigma_ref[1, :, :, lanes].reshape(2 * ORB, TB * ORB), pick)
        own = iota((2 * ORB, 128), 1) // ORB == iota((2 * ORB, 128), 0) % 4
        fold = one_hot(iota((DIAG, 2 * ORB), 1) // 4 == iota((DIAG, 2 * ORB), 0))
        diag = dot(fold, jnp.where(own, tiled, 0.0).astype(BF)) * 0.5
        own_ref[SPAN:, :] = diag
        other_ref[SPAN:, :] = diag.astype(BF)

    for k in range(ROWS):
        chunks[k].wait()
        if k + 6 < ROWS:
            chunks[k + 6].start()
        for kind in range(2):
            part = dot(left_ref[k], hist_ref[k, kind].reshape(2 * TB * ORB, hist_ref.shape[-1]))
            if k == 0:
                acc_ref[kind] = part
            else:
                acc_ref[kind] += part

    @pl.when(holds_now)
    def _():
        at = current % TB
        real, imag = prop_ref[0], prop_ref[1]
        by_real = jnp.concatenate([real, imag], axis=0)
        by_imag = jnp.concatenate([-imag, real], axis=0)
        for kind in range(2):
            acc_ref[kind, : 2 * ORB] += dot(by_real, hist_ref[chunk_now, kind, 0, at]) + dot(
                by_imag, hist_ref[chunk_now, kind, 1, at]
            )

    other_ref[:SPAN, :] = acc_ref[1 - core].T.astype(BF)
    own_ref[:SPAN, :] = acc_ref[core].T


def join_kernel(own_ref, other_ref, out_ref):
    total = (own_ref[...] + other_ref[...].astype(F32)).astype(BF)
    for part in range(PARTS):
        for blk in range(2):
            first = (blk * PARTS + part) * 16
            out_ref[part, blk * 16 : blk * 16 + 16, :] = total[first : first + 16]
        out_ref[part, DATA:, :] = total[SPAN:]


def finish_kernel(in_ref, prop_ref, rows_ref, mirror_ref):
    sums = []
    for x in range(XS):
        total = in_ref[x, :DATA].astype(F32)
        for r in range(1, YS):
            total += in_ref[r * XS + x, :DATA].astype(F32)
        sums.append(total)
    total = jnp.concatenate(sums, axis=0)
    packed = in_ref[0, DATA:].astype(F32)
    for r in range(1, YS):
        packed += in_ref[r * XS, DATA:].astype(F32)
    lane = iota((ORB, 128), 1)
    left, right = lane < ORB, (lane >= ORB) & (lane < 2 * ORB)
    nothing = jnp.zeros((2 * ORB, 128), F32)

    def matrix(upper_left, upper_right, lower_left, lower_right):
        upper = jnp.where(left, upper_left, jnp.where(right, upper_right, 0.0))
        lower = jnp.where(left, lower_left, jnp.where(right, lower_right, 0.0))
        return jnp.concatenate([nothing, upper, lower], axis=0).astype(BF)

    tile = one_hot(iota((ORB, 128), 0) == iota((ORB, 128), 1) % ORB)
    real, imag = dot(prop_ref[0], tile), dot(prop_ref[1], tile)
    propagate = matrix(real, -imag, imag, real)
    spread = one_hot(iota((2 * ORB, DIAG), 0) // 4 == iota((2 * ORB, DIAG), 1))
    own = iota((2 * ORB, 128), 1) // ORB == iota((2 * ORB, 128), 0) % 4
    wide = jnp.where(own, dot(spread, packed.astype(BF)), 0.0).astype(BF)
    wrap = one_hot(iota((128, 128), 0) % ORB == iota((128, 128), 1) % ORB)
    diag = dot(wide, wrap)
    d_real, d_imag = diag[:ORB], diag[ORB:]
    turn = matrix(d_imag, d_real, -d_real, d_imag)
    low = total.astype(BF)
    new = (total + dot_nt(low, propagate) + dot_nt(low, turn)).astype(BF)
    rows_ref[...] = new
    size = XS * DATA
    lane_block = iota((size, 128), 1) // ORB
    place = iota((size, 128), 0) % 4
    signed = jnp.where(lane_block % 2 == 0, -new.astype(F32), new.astype(F32))
    result = jnp.where(lane_block == place, signed, 0.0)
    for d in range(1, 4):
        moved = jnp.where(lane_block == place, pltpu.roll(signed, 128 - ORB * d, 1), 0.0)
        result += jnp.where(
            place >= d, pltpu.roll(moved, d, 0), pltpu.roll(moved, size + d - 4, 0)
        )
    result = result.astype(BF)
    for z in range(ZS):
        mirror_ref[z] = result


def select_kernel(map_ref, blocks_ref, rows_ref, out_ref):
    for r in range(ROWS):
        for j in range(TB):
            block = map_ref[r * TB + j]
            column = block // 2
            start = pl.multiple_of(column // ZS * DATA + block % 2 * 16, 16)
            piece = blocks_ref[column % ZS, pl.ds(start, 16), :]
            for x in range(XS):
                out_ref[r * XS + x, j * 16 : j * 16 + 16, :] = piece
        for x in range(XS):
            out_ref[r * XS + x, 128:, :] = rows_ref[x * DATA : x * DATA + DATA, :]


def place_kernel(in_ref, rows_hbm, mirror_hbm, mixed_ref, tall_ref, rows_ref, mirror_ref, rows_sem, mirror_sem):
    copies = []

    def send(source, target, semaphore):
        copies.append(pltpu.make_async_copy(source, target, semaphore))
        copies[-1].start()

    for kind in range(2):
        for pair in range(4):
            for h in range(2):
                for half in range(2):
                    j = pair * 2 + half
                    for tm in range(TB):
                        mixed_ref[kind, h, pair, pl.ds(half * 8 + tm, 16, stride=16), :] = in_ref[
                            tm // 2, kind, tm % 2 * 2 + h, j * 16 : j * 16 + 16, :
                        ].astype(F32)
                for q in range(4):
                    for g in range(4):
                        first = (q * 4 + g) * 16
                        lanes = slice((h * 4 + q) * 128, (h * 4 + q) * 128 + 128)
                        mirror_ref[g // 2, kind, g % 2, pair * 16 : pair * 16 + 16, lanes] = mixed_ref[
                            kind, h, pair, first : first + 16, :
                        ].astype(BF)
            own = (slice(None), kind, slice(None), pl.ds(pair * 16, 16))
            send(mirror_ref.at[own], mirror_hbm.at[own], mirror_sem.at[kind, pair])
    for kind in range(2):
        for blk in range(2):
            for part in range(PARTS):
                first = (blk * PARTS + part) * 16
                tall_ref[kind, first : first + 16, :] = in_ref[
                    part // XS, kind, part % XS, 128 + blk * 16 : 144 + blk * 16, :
                ].astype(F32)
        wide = tall_ref[kind].T
        for g in range(4):
            rows_ref[g // 2, kind, g % 2] = wide[g * ORB : g * ORB + ORB, :]
        send(rows_ref.at[:, kind], rows_hbm.at[:, kind], rows_sem.at[kind])
    for copy in copies:
        copy.wait()


def per_device(history, sigma_rows, propagator, block_map, step_index):
    smem = pl.BlockSpec(memory_space=pltpu.SMEM)
    vmem = pl.BlockSpec(memory_space=pltpu.VMEM)
    columns = history.shape[4]
    hbm = pl.BlockSpec(memory_space=pltpu.HBM)
    small = pltpu.CompilerParams(vmem_limit_bytes=16 << 20)
    inputs = (block_map, history, sigma_rows, propagator)
    other, own, kept_map = pl.pallas_call(
        product_kernel,
        in_specs=[smem] + [hbm] * 4,
        out_specs=[vmem, vmem, smem],
        out_shape=[
            jax.ShapeDtypeStruct((SPAN + DIAG, 128), BF),
            jax.ShapeDtypeStruct((SPAN + DIAG, 128), F32),
            pltpu.SMEM(block_map.shape, jnp.int32),
        ],
        scratch_shapes=[
            pltpu.VMEM((ROWS, 2, 2, TB, ORB, columns), BF),
            pltpu.VMEM(sigma_rows.shape, BF),
            pltpu.VMEM(propagator.shape, BF),
            pltpu.VMEM((ROWS, 128, 2 * TB * ORB), BF),
            pltpu.VMEM((2, 128, columns), F32),
            pltpu.SemaphoreType.DMA((ROWS,)),
            pltpu.SemaphoreType.DMA((3,)),
        ],
        compiler_params=pltpu.CompilerParams(vmem_limit_bytes=40 << 20),
        name="products",
    )(step_index, *(pltpu.with_memory_space_constraint(a, pltpu.HBM) for a in inputs))
    other = lax.ppermute(other, "core", ((0, 1), (1, 0)))
    partial = pl.pallas_call(
        join_kernel,
        in_specs=[vmem] * 2,
        out_specs=vmem,
        out_shape=jax.ShapeDtypeStruct((PARTS, DATA + DIAG, 128), BF),
        compiler_params=small,
        name="join",
    )(own, other)
    partial = lax.all_to_all(partial, ("y", "x"), 0, 0, tiled=True)
    new, copies = pl.pallas_call(
        finish_kernel,
        in_specs=[vmem, vmem],
        out_specs=[vmem, vmem],
        out_shape=[
            jax.ShapeDtypeStruct((XS * DATA, 128), BF),
            jax.ShapeDtypeStruct((ZS, XS * DATA, 128), BF),
        ],
        compiler_params=pltpu.CompilerParams(vmem_limit_bytes=16 << 20),
        name="finish",
    )(partial, propagator)
    blocks = lax.all_to_all(copies, "z", 0, 0, tiled=True)
    back = pl.pallas_call(
        select_kernel,
        in_specs=[smem, vmem, vmem],
        out_specs=vmem,
        out_shape=jax.ShapeDtypeStruct((SLICES, BACK, 128), BF),
        compiler_params=pltpu.CompilerParams(vmem_limit_bytes=16 << 20),
        name="select",
    )(kept_map, blocks, new)
    back = lax.all_to_all(back, ("y", "core", "x"), 0, 0, tiled=True)
    back = back.reshape(YS, 2, XS, BACK, 128)
    rows_shape = (2, 2, 2, ORB, columns)
    mirror_shape = (2, 2, 2, ROWS * TB, ORB * ORB)
    new_rows, mirror = pl.pallas_call(
        place_kernel,
        in_specs=[vmem],
        out_specs=[pl.BlockSpec(memory_space=pl.ANY)] * 2,
        out_shape=[jax.ShapeDtypeStruct(rows_shape, F32), jax.ShapeDtypeStruct(mirror_shape, BF)],
        scratch_shapes=[
            pltpu.VMEM((2, 2, 4, 272, 128), F32),
            pltpu.VMEM((2, columns, 128), F32),
            pltpu.VMEM(rows_shape, F32),
            pltpu.VMEM(mirror_shape, BF),
            pltpu.SemaphoreType.DMA((2,)),
            pltpu.SemaphoreType.DMA((2, 4)),
        ],
        compiler_params=small,
        name="place",
    )(back)
    return new_rows, mirror


def solution(mesh):
    split = Mesh(mesh.devices.reshape(YS, 2, XS, ZS), ("y", "core", "x", "z"))
    row = ("y", "core")
    column = ("x", "z")
    return jax.shard_map(
        per_device,
        mesh=split,
        in_specs=(P(None, None, row, None, column), P(None, None, None, row), P(), P(), P()),
        out_specs=(P(None, None, None, None, column), P(None, None, None, row, None)),
        check_vma=False,
    )
```
